512 devices in a mesh: section: 16 (over x, z_lo, core), dp: 32 (over y, z_hi).
Axes of the slice: x: 4, y: 8, z: 8 (z_hi: 4, z_lo: 2; z = z_hi * 2 + z_lo), core: 2. Of those that a mesh axis runs over, the one named last changes fastest.
Arguments:
- inputs: bfloat16 [4, 1024, 2048], P(None, 'dp'), may hold values from -6 to 6
- upstream: bfloat16 [4, 1024, 2048], P(None, 'dp'), may hold values from -6 to 6
- segments: int32 [4, 1024], P(None, 'dp'), may hold values from 0 to 127, never falling along the last dimension, each value on 1 to 16 neighbouring positions
- gains: float32 [16, 2048], P('section'), may hold values from 0.5 to 1.5
- master: float32 [16, 2048, 1024], P('section', 'dp'), may hold values from -0.125 to 0.125
- moment: float32 [16, 2048, 1024], P('section', 'dp'), may hold values from -0.15625 to 0.15625
- second: float32 [16, 2048, 1024], P('section', 'dp'), may hold values from 1e-05 to 0.001
Outputs:
- new_master: float32 [16, 2048, 1024], P('section', 'dp')
- new_moment: float32 [16, 2048, 1024], P('section', 'dp')
- new_second: float32 [16, 2048, 1024], P('section', 'dp')
- replica: bfloat16 [16, 2048, 1024], P('section', 'dp')
The draws below stay inside these ranges and needn't reach their ends.
Inputs may be any that keep to these rules, and one draw needn't show every extreme that they name: `segments`: segment numbers never fall along a micro-batch; each segment holds 1 to 16 positions, one exactly 16.
All inputs are finite; a program needn't handle non-finite values.
Results may differ from the reference program's by a relative error of at most 0.0065.
Values may be sent and summed in bfloat16 or wider, within the bound.
No kernel may reach another device: no remote copies, remote signals or barrier semaphores. Data moves between devices by JAX's collectives and lax.ppermute only.
A program may use at most 64 MiB of HBM per device.

```python
import math
import jax
import jax.numpy as jnp
import numpy as np
from jax import lax

D = 2048
KVW = 512
HEAD = 128
MICRO = 4
SEQ = 32
LAYERS = 16
TOKENS = 1024
N_DP = 32


def block_scale(rng, dims, pieces, smallest, top_value):
    loudness = 1.0
    for axis_at, shards_of in pieces:
        steps = jax.random.uniform(jax.random.fold_in(jax.random.fold_in(rng, 6), axis_at), (shards_of,), jnp.float32, smallest / len(pieces), top_value / len(pieces))
        loudness = loudness * jnp.repeat(jnp.exp(steps), dims[axis_at] // shards_of).reshape((-1,) + (1,) * (len(dims) - 1 - axis_at))
    return loudness


def length_profile(amount, total, most, slope):
    portions = [(1 << 20) // math.isqrt(standing ** slope) + 1 for standing in range(2, amount + 1)]
    surplus, given = total - most - (amount - 1), [1] * (amount - 1)
    while surplus > 0:
        free = [i for i in range(amount - 1) if given[i] < most]
        mass, remaining = sum([portions[i] for i in free]), surplus
        for i in free:
            addition = min(most - given[i], max(1, remaining * portions[i] // mass), surplus)
            given[i] = given[i] + addition
            surplus = surplus - addition
    return np.array([most] + given)


def ragged(rng, number_of, total, bound, lean):
    if number_of == 2:
        one = jax.random.randint(rng, (), max(1, total - bound), min(bound, total - 1) + 1)
        return jnp.stack([one, total - one])
    lengths = jnp.asarray(length_profile(number_of, total, bound, lean), jnp.int32)
    pairs = (number_of - 1) // 2
    donor, taker = lengths[1:1 + 2 * pairs:2], lengths[2:2 + 2 * pairs:2]
    slack = jnp.minimum(donor - 1, bound - taker)
    shifted = jax.random.randint(jax.random.fold_in(rng, 1), (pairs,), 0, 1 << 20) % (slack + 1)
    lengths = lengths.at[1:1 + 2 * pairs:2].set(donor - shifted).at[2:2 + 2 * pairs:2].set(taker + shifted)
    return lengths[jax.random.permutation(jax.random.fold_in(rng, 2), number_of)]


def centred(stream_key, extent, spread, bound, shards=(), dtype=jnp.bfloat16):
    level = block_scale(stream_key, extent, shards, -0.22, 0.18) if shards else 1.0
    entries = jax.random.normal(stream_key, extent, jnp.float32) * spread * level
    return jnp.minimum(jnp.maximum(entries, -bound), bound).astype(dtype)


def setup_inputs(seed: int = 0) -> dict:
    arg_keys = jax.random.split(jax.random.key(seed), 8)
    inputs = centred(arg_keys[0], (MICRO, TOKENS, D), 1.0, 6.0, ((1, 32),))
    upstream = centred(arg_keys[1], (MICRO, TOKENS, D), 1.0, 6.0, ((1, 32),))
    segments = jax.vmap(lambda own: jnp.searchsorted(jnp.cumsum(ragged(own, TOKENS // 8, TOKENS, 16, 1)), jnp.arange(TOKENS), side="right"))(jax.random.split(arg_keys[2], MICRO)).reshape((MICRO, TOKENS)).astype(jnp.int32)
    gains = jnp.clip(1.0 + 0.1 * jax.random.normal(arg_keys[3], (LAYERS, D), jnp.float32), 0.5, 1.5)
    master = centred(arg_keys[4], (LAYERS, D, 2 * KVW), D ** -0.5, 0.125, ((0, 16), (1, 32)), jnp.float32)
    moment = centred(arg_keys[5], (LAYERS, D, 2 * KVW), 0.01, 0.15625, ((0, 16), (1, 32)), jnp.float32)
    second = jnp.clip(jnp.exp(math.log(0.001) - 4.6051703 * jax.random.uniform(arg_keys[6], (LAYERS, D, 2 * KVW), jnp.float32) ** block_scale(arg_keys[6], (LAYERS, D, 2 * KVW), ((0, 16), (1, 32)), -0.2, 0.2)), 9.999999747378752e-06, 0.001)
    return dict(inputs=inputs, upstream=upstream, segments=segments, gains=gains, master=master, moment=moment, second=second)


def normed(xf, gain):
    return xf * lax.rsqrt(lax.optimization_barrier(jnp.mean(xf * xf, axis=-1, keepdims=True)) + 1e-05) * gain

def attend(x, h, kv, seg):
    length = x.shape[0]
    width = kv.shape[1] // 2
    kv_heads = width // HEAD
    groups = h.shape[1] // HEAD // kv_heads
    query = h.astype(jnp.float32).reshape(length, kv_heads, groups, HEAD)
    keys = kv[:, :width].astype(jnp.float32).reshape(length, kv_heads, HEAD)
    values = kv[:, width:].astype(jnp.float32).reshape(length, kv_heads, HEAD)
    scores = jnp.einsum('qhgd,khd->hgqk', query, keys) * HEAD ** (-0.5)
    place = jnp.arange(length)
    allowed = (place[:, None] >= place[None, :]) & (seg[:, None] == seg[None, :])
    scores = jnp.where(allowed, scores, -1e+30)
    probs = jax.nn.softmax(scores, axis=-1).astype(jnp.bfloat16)
    mixed = jnp.einsum('hgqk,khd->qhgd', probs.astype(jnp.float32), values).reshape(length, -1)
    return (x.astype(jnp.float32) + mixed).astype(jnp.bfloat16)

def forward(x, gain, w, seg):
    h = normed(x.astype(jnp.float32), gain).astype(jnp.bfloat16)
    kv = jnp.dot(h, w, preferred_element_type=jnp.float32).astype(jnp.bfloat16)
    return attend(x, h, kv, seg)

def backward(x, gain, w, seg, dy):
    hf, pull_norm = jax.vjp(lambda v: normed(v, gain), x.astype(jnp.float32))
    hb = hf.astype(jnp.bfloat16)
    kv = jnp.dot(hb, w, preferred_element_type=jnp.float32).astype(jnp.bfloat16)
    _, pull = jax.vjp(lambda a, b, c: attend(a, b, c, seg), x, hb, kv)
    dx_direct, dh_attn, dkv = pull(dy)
    dh = dh_attn.astype(jnp.float32) + lax.dot_general(dkv, w, (((1,), (1,)), ((), ())), preferred_element_type=jnp.float32)
    dx = (dx_direct.astype(jnp.float32) + pull_norm(dh)[0]).astype(jnp.bfloat16)
    return (dx, hb, dkv)

def reference(inputs, upstream, segments, gains, master, moment, second):
    seqs = inputs.reshape(MICRO, N_DP, SEQ, D)
    segs = segments.reshape(MICRO, N_DP, SEQ)
    grads_in = upstream.reshape(MICRO, N_DP, SEQ, D)
    weights = master.astype(jnp.bfloat16)
    fwd_all = jax.vmap(jax.vmap(forward, in_axes=(0, None, None, 0)), in_axes=(0, None, None, 0))
    bwd_all = jax.vmap(jax.vmap(backward, in_axes=(0, None, None, 0, 0)), in_axes=(0, None, None, 0, 0))

    def fstep(x, layer):
        gain, w = layer
        return (fwd_all(x, gain, w, segs), x)
    _, stored = lax.scan(fstep, seqs, (gains, weights))

    def bstep(dy, layer):
        x, gain, w = layer
        dx, hb, dkv = bwd_all(x, gain, w, segs, dy)
        partial_value = jnp.einsum('mpsd,mpse->pde', hb.astype(jnp.float32), dkv.astype(jnp.float32))
        rounded = lax.optimization_barrier(partial_value.astype(jnp.bfloat16)).astype(jnp.float32)
        return (dx, lax.optimization_barrier(jnp.sum(rounded, axis=0)))
    _, grads = lax.scan(bstep, grads_in, (stored, gains, weights), reverse=True)
    total = jnp.sum(grads * grads)
    factor = jnp.minimum(1.0, 0.01 / jnp.sqrt(total / grads.size))
    scaled = grads * factor
    new_moment = 0.9 * moment + 0.1 * scaled
    new_second = 0.95 * second + 0.05 * scaled * scaled
    new_master = master - 0.002 * new_moment / (jnp.sqrt(new_second) + 1e-08)
    replica = jnp.roll(new_master.astype(jnp.bfloat16), -1, axis=0)
    return (new_master, new_moment, new_second, replica)
```

```python
import functools

import jax
import jax.numpy as jnp
from jax import lax
from jax.experimental import pallas as pl
from jax.experimental.pallas import tpu as pltpu
from jax.sharding import Mesh
from jax.sharding import PartitionSpec as P

HEAD = 128
X, ZL, C, Y, ZH = 4, 2, 2, 8, 4
AXES = ("x", "zl", "c", "y", "zh")
SECTION = ("x", "zl", "c")
DP = ("y", "zh")
LAYERS = ZL * C
RING = 8
OFFSETS = (0, 1, -1, 2, -2, 3, -3, 4)
KV_HEADS = 4
GROUPS = 4
F32 = jnp.float32
BF16 = jnp.bfloat16


def flat(x, zl, c, y, zh):
    return (((x * ZL + zl) * C + c) * Y + y) * ZH + zh


def everywhere(target):
    pairs = []
    for x in range(X):
        for zl in range(ZL):
            for c in range(C):
                for y in range(Y):
                    for zh in range(ZH):
                        pairs.append((flat(x, zl, c, y, zh), flat(*target(x, zl, c, y, zh))))
    return pairs


def swap_route(bit):
    def target(x, zl, c, y, zh):
        if c == 1:
            return (x, zl, c, y ^ (1 << bit), zh)
        if bit == 0:
            return (x, zl ^ 1, c, y, zh)
        return (x, zl, c, y, zh ^ (1 << (bit - 1)))

    return everywhere(target)


def ring_route(step):
    def target(x, zl, c, y, zh):
        if c == 0:
            return (x, zl, c, (y + step) % Y, zh)
        z = (2 * zh + zl + step) % (ZL * ZH)
        return (x, z % 2, c, y, z // 2)

    return everywhere(target)


def gathered_weights(own):
    c, y = lax.axis_index("c"), lax.axis_index("y")
    zl, zh = lax.axis_index("zl"), lax.axis_index("zh")
    rows, cols = own.shape
    bits = (
        jnp.where(c == 1, y // 4, zh // 2),
        jnp.where(c == 1, (y // 2) % 2, zh % 2),
        jnp.where(c == 1, y % 2, zl),
    )
    piece = own[None]
    for bit, mine, axis in ((2, bits[0], 0), (1, bits[1], 1), (0, bits[2], 0)):
        other = lax.ppermute(piece, AXES, swap_route(bit))
        low, high = jnp.where(mine == 0, piece, other), jnp.where(mine == 0, other, piece)
        if axis == 0:
            piece = jnp.concatenate([low, high], axis=0)
        else:
            piece = jnp.stack([low, high], axis=1).reshape(-1, rows, cols)
    pieces = [piece]
    up = down = piece
    for step in range(1, 5):
        up = lax.ppermute(up, AXES, ring_route(1))
        pieces.append(up)
        if step < 4:
            down = lax.ppermute(down, AXES, ring_route(-1))
            pieces.append(down)
    others = [lax.ppermute(p, "c", [(0, 1), (1, 0)]) for p in pieces]
    return pieces + others


def fetch_weights(pieces, w, sems):
    c, y = lax.axis_index("c"), lax.axis_index("y")
    z = 2 * lax.axis_index("zh") + lax.axis_index("zl")

    def start(first, second):
        for i, offset in enumerate(OFFSETS):
            there = lax.rem(y - offset + 2 * RING, RING)
            for low in range(2):
                pltpu.make_async_copy(
                    first[i].at[pl.ds(4 * low, 4)],
                    w.at[2 * low, there // 2, lax.rem(there, 2)],
                    sems.at[2 * low],
                ).start()
        for i, offset in enumerate(OFFSETS):
            there = lax.rem(z - offset + 2 * RING, RING)
            layer = 2 * lax.rem(there, 2) + 1
            for low in range(2):
                pltpu.make_async_copy(
                    second[i].at[pl.ds(4 * low, 4)],
                    w.at[layer, :, low, there // 2],
                    sems.at[layer],
                ).start()

    @pl.when(c == 0)
    def _():
        start(pieces[:RING], pieces[RING:])

    @pl.when(c == 1)
    def _():
        start(pieces[RING:], pieces[:RING])


def wait_weights(w, sems, layer):
    pltpu.make_async_copy(w.at[layer], w.at[layer], sems.at[layer]).wait()


def cols(index):
    return pl.ds(index * HEAD, HEAD)


def stacked(ref, layer, group):
    parts = [ref[layer, :, cols(group * GROUPS + a)] for a in range(GROUPS)]
    return jnp.concatenate(parts, axis=0)


def forward_kernel(x_ref, gain_ref, mask_ref, *rest):
    pieces = rest[: 2 * RING]
    y_ref, xs_ref, h_ref, kv_ref, p_ref, w, sems = rest[2 * RING :]
    fetch_weights(pieces, w, sems)
    length, width = x_ref.shape
    y_ref[...] = x_ref[...]

    @pl.loop(0, LAYERS)
    def _(layer):
        xs_ref[layer] = y_ref[...]
        xf = y_ref[...].astype(F32)
        scale = lax.rsqrt(jnp.mean(xf * xf, axis=-1, keepdims=True) + 1e-05)
        h_ref[layer] = (xf * scale * gain_ref[layer]).astype(BF16)
        wait_weights(w, sems, layer)
        whole = w[layer].reshape(width, -1)
        kv_ref[layer] = jnp.dot(h_ref[layer], whole, preferred_element_type=F32).astype(BF16)
        for g in range(KV_HEADS):
            query = stacked(h_ref, layer, g)
            key = kv_ref[layer, :, cols(g)]
            value = kv_ref[layer, :, cols(KV_HEADS + g)]
            s = lax.dot_general(key, query, (((1,), (1,)), ((), ())), preferred_element_type=F32)
            s = jnp.where(mask_ref[...] > 0, s * HEAD ** (-0.5), -1e30)
            e = jnp.exp(s - jnp.max(s, axis=0, keepdims=True))
            p = e / jnp.sum(e, axis=0, keepdims=True)
            p_ref[layer, :, cols(g)] = p
            o = lax.dot_general(
                p.astype(BF16), value, (((0,), (0,)), ((), ())), preferred_element_type=F32
            )
            for a in range(GROUPS):
                at = cols(g * GROUPS + a)
                y_ref[:, at] = (
                    xs_ref[layer, :, at].astype(F32) + o[a * length : (a + 1) * length]
                ).astype(BF16)


def backward_kernel(dy_ref, gain_ref, xs_ref, h_ref, kv_ref, p_ref, *rest):
    pieces = rest[: 2 * RING]
    dx_ref, dkv_ref, w, sems, dh_ref = rest[2 * RING :]
    fetch_weights(pieces, w, sems)
    length, width = dy_ref.shape
    dx_ref[...] = dy_ref[...]

    @pl.loop(0, LAYERS)
    def _(turn):
        layer = LAYERS - 1 - turn
        for g in range(KV_HEADS):
            query = stacked(h_ref, layer, g)
            key = kv_ref[layer, :, cols(g)]
            value = kv_ref[layer, :, cols(KV_HEADS + g)]
            p = p_ref[layer, :, cols(g)]
            do = jnp.concatenate(
                [dx_ref[:, cols(g * GROUPS + a)] for a in range(GROUPS)], axis=0
            )
            dv = jnp.dot(p.astype(BF16), do, preferred_element_type=F32)
            dp = lax.dot_general(value, do, (((1,), (1,)), ((), ())), preferred_element_type=F32)
            ds = p * (dp - jnp.sum(p * dp, axis=0, keepdims=True)) * HEAD ** (-0.5)
            ds = ds.astype(BF16)
            dk = jnp.dot(ds, query, preferred_element_type=F32)
            dq = lax.dot_general(ds, key, (((0,), (0,)), ((), ())), preferred_element_type=F32)
            dkv_ref[layer, :, cols(g)] = dk.astype(BF16)
            dkv_ref[layer, :, cols(KV_HEADS + g)] = dv.astype(BF16)
            for a in range(GROUPS):
                dh_ref[:, cols(g * GROUPS + a)] = dq[a * length : (a + 1) * length]
        wait_weights(w, sems, layer)
        whole = w[layer].reshape(width, -1)
        dh = dh_ref[...] + lax.dot_general(
            dkv_ref[layer], whole, (((1,), (1,)), ((), ())), preferred_element_type=F32
        )
        xf = xs_ref[layer].astype(F32)
        scale = lax.rsqrt(jnp.mean(xf * xf, axis=-1, keepdims=True) + 1e-05)
        gd = dh * gain_ref[layer]
        along = jnp.mean(xf * gd, axis=-1, keepdims=True) * (scale * scale * scale)
        dx_ref[...] = (dx_ref[...].astype(F32) + (gd * scale - xf * along)).astype(BF16)


def weights_scratch(pieces):
    rows, columns = pieces[0].shape[1:]
    return [
        pltpu.VMEM((LAYERS, Y // 2, 2, ZH, rows, columns), BF16),
        pltpu.SemaphoreType.DMA((LAYERS,)),
    ]


VMEM = pl.BlockSpec(memory_space=pltpu.VMEM)
ANY = pl.BlockSpec(memory_space=pl.ANY)
PARAMS = dict(vmem_limit_bytes=48 * 1024 * 1024)


def run_forward(x, gains, mask, pieces):
    length, width = x.shape
    columns = pieces[0].shape[2]
    return pl.pallas_call(
        forward_kernel,
        out_shape=(
            jax.ShapeDtypeStruct((length, width), BF16),
            jax.ShapeDtypeStruct((LAYERS, length, width), BF16),
            jax.ShapeDtypeStruct((LAYERS, length, width), BF16),
            jax.ShapeDtypeStruct((LAYERS, length, columns), BF16),
            jax.ShapeDtypeStruct((LAYERS, length, KV_HEADS * HEAD), F32),
        ),
        in_specs=[VMEM] * 3 + [ANY] * (2 * RING),
        out_specs=(VMEM,) * 5,
        scratch_shapes=weights_scratch(pieces),
        compiler_params=pltpu.CompilerParams(**PARAMS),
        name="stage_forward",
    )(x, gains, mask, *pieces)


def run_backward(dy, gains, saved, pieces):
    length, width = dy.shape
    columns = pieces[0].shape[2]
    return pl.pallas_call(
        backward_kernel,
        out_shape=(
            jax.ShapeDtypeStruct((length, width), BF16),
            jax.ShapeDtypeStruct((LAYERS, length, columns), BF16),
        ),
        in_specs=[VMEM] * 6 + [ANY] * (2 * RING),
        out_specs=(VMEM,) * 2,
        scratch_shapes=weights_scratch(pieces) + [pltpu.VMEM((length, width), F32)],
        compiler_params=pltpu.CompilerParams(**PARAMS),
        name="stage_backward",
    )(dy, gains, *saved, *pieces)


def exchange(block, axes):
    return lax.all_to_all(block, axes, split_axis=0, concat_axis=0, tiled=True)


def total_of(value):
    for axes, count in ((DP, Y * ZH), (SECTION, X * ZL * C)):
        sent = jnp.broadcast_to(value.reshape(1, 1), (count, 128))
        value = jnp.sum(exchange(sent, axes)[:, 0])
    return value


def body(inputs, upstream, segments, gains, master, moment, second):
    stage = lax.axis_index("x")
    which = lax.axis_index("zl") * C + lax.axis_index("c")
    length, width = inputs.shape[1:]
    rows, columns = master.shape[1:]

    pieces = gathered_weights(master[0].astype(BF16))
    plane_gains = lax.all_gather(gains, ("zl", "c"), axis=0)
    seg = lax.dynamic_index_in_dim(segments, which, 0, keepdims=False)
    place = jnp.arange(length)
    allowed = (place[None, :] >= place[:, None]) & (seg[None, :] == seg[:, None])
    mask = jnp.tile(allowed.astype(F32), (1, GROUPS))
    first = lax.dynamic_index_in_dim(inputs, which, 0, keepdims=False)
    last = lax.dynamic_index_in_dim(upstream, which, 0, keepdims=False)

    held = first
    for turn in range(X):
        y, *saved = run_forward(held, plane_gains, mask, pieces)
        if turn < X - 1:
            arrived = lax.ppermute(y, "x", [(turn, turn + 1)])
            held = jnp.where(stage == turn + 1, arrived, held)
    h = saved[1]
    layer_h = exchange(h, ("zl", "c")).reshape(LAYERS * length, width)
    all_h = lax.all_gather(layer_h, "y", axis=0, tiled=True)

    held = last
    for turn in range(X):
        dx, dkv = run_backward(held, plane_gains, saved, pieces)
        if turn < X - 1:
            here = X - 1 - turn
            arrived = lax.ppermute(dx, "x", [(here, here - 1)])
            held = jnp.where(stage == here - 1, arrived, held)

    sent = dkv.reshape(LAYERS, length, Y, columns // Y).transpose(0, 2, 1, 3)
    sent = sent.reshape(LAYERS * Y, length, columns // Y)
    got = exchange(sent, ("zl", "c", "y")).reshape(LAYERS, Y, length, columns // Y)
    tokens = got.transpose(1, 0, 2, 3).reshape(Y * LAYERS * length, columns // Y)
    partial = lax.dot_general(
        all_h, tokens, (((0,), (0,)), ((), ())), preferred_element_type=F32
    ).astype(BF16)
    got = exchange(partial.reshape(Y * ZH, rows, columns // Y), DP)
    grad = jnp.sum(got.reshape(Y, ZH, rows, columns // Y).astype(F32), axis=1)
    grad = grad.transpose(1, 0, 2).reshape(rows, columns)

    total = total_of(jnp.sum(grad * grad))
    entries = X * ZL * C * Y * ZH * grad.size
    factor = jnp.minimum(1.0, 0.01 / jnp.sqrt(total / entries))
    scaled = grad * factor
    new_moment = 0.9 * moment[0] + 0.1 * scaled
    new_second = 0.95 * second[0] + 0.05 * scaled * scaled
    new_master = master[0] - 0.002 * new_moment / (jnp.sqrt(new_second) + 1e-08)
    sections = X * ZL * C
    route = [((i + 1) % sections, i) for i in range(sections)]
    replica = lax.ppermute(new_master.astype(BF16), SECTION, route)
    return (new_master[None], new_moment[None], new_second[None], replica[None])


def solution(mesh):
    fine = Mesh(mesh.devices.reshape(X, ZL, C, Y, ZH), AXES)
    state = P(SECTION, DP, None)
    return jax.shard_map(
        body,
        mesh=fine,
        in_specs=(
            P(None, DP, None),
            P(None, DP, None),
            P(None, DP),
            P(SECTION, None),
            state,
            state,
            state,
        ),
        out_specs=(state,) * 4,
        check_vma=False,
    )
```

```python
import functools

import jax
import jax.numpy as jnp
from jax import lax
from jax.experimental import pallas as pl
from jax.experimental.pallas import tpu as pltpu
from jax.sharding import Mesh
from jax.sharding import PartitionSpec as P

HEAD = 128
X, ZL, C, Y, ZH = 4, 2, 2, 8, 4
AXES = ("x", "zl", "c", "y", "zh")
SECTION = ("x", "zl", "c")
DP = ("y", "zh")
LAYERS = ZL * C
RING = 8
PIECES = RING + 1
OFFSETS = (0, 1, -1, 2, -2, 3, -3, 4)
KV_HEADS = 4
GROUPS = 4
F32 = jnp.float32
BF16 = jnp.bfloat16


def flat(x, zl, c, y, zh):
    return (((x * ZL + zl) * C + c) * Y + y) * ZH + zh


def everywhere(target):
    pairs = []
    for x in range(X):
        for zl in range(ZL):
            for c in range(C):
                for y in range(Y):
                    for zh in range(ZH):
                        pairs.append((flat(x, zl, c, y, zh), flat(*target(x, zl, c, y, zh))))
    return pairs


def swap_route(bit):
    def target(x, zl, c, y, zh):
        if c == 1:
            return (x, zl, c, y ^ (1 << bit), zh)
        if bit == 0:
            return (x, zl ^ 1, c, y, zh)
        return (x, zl, c, y, zh ^ (1 << (bit - 1)))

    return everywhere(target)


def ring_route(step):
    def target(x, zl, c, y, zh):
        if c == 0:
            return (x, zl, c, (y + step) % Y, zh)
        z = (2 * zh + zl + step) % (ZL * ZH)
        return (x, z % 2, c, y, z // 2)

    return everywhere(target)


def gathered_weights(own, beside):
    c, y = lax.axis_index("c"), lax.axis_index("y")
    zl, zh = lax.axis_index("zl"), lax.axis_index("zh")
    rows, cols = own.shape
    bits = (
        jnp.where(c == 1, y // 4, zh // 2),
        jnp.where(c == 1, (y // 2) % 2, zh % 2),
        jnp.where(c == 1, y % 2, zl),
    )
    piece = own[None]
    for bit, mine, axis in ((2, bits[0], 0), (1, bits[1], 1), (0, bits[2], 0)):
        other = lax.ppermute(piece, AXES, swap_route(bit))
        low, high = jnp.where(mine == 0, piece, other), jnp.where(mine == 0, other, piece)
        if axis == 0:
            piece = jnp.concatenate([low, high], axis=0)
        else:
            piece = jnp.stack([low, high], axis=1).reshape(-1, rows, cols)
    pieces = [piece]
    up = down = piece
    for step in range(1, 4):
        if step == 2:
            up, down, ready = lax.optimization_barrier((up, down, beside(piece)))
        up = lax.ppermute(up, AXES, ring_route(1))
        down = lax.ppermute(down, AXES, ring_route(-1))
        pieces += [up, down]
    pieces.append(lax.ppermute(up[:4], AXES, ring_route(1)))
    pieces.append(lax.ppermute(down[4:], AXES, ring_route(-1)))
    others = [lax.ppermute(p, "c", [(0, 1), (1, 0)]) for p in pieces]
    return pieces + others, ready


def half(pieces, index, low):
    if index == RING - 1:
        return pieces[index + low]
    return pieces[index].at[pl.ds(4 * low, 4)]


def fetch_weights(pieces, w, sems, order):
    c, y = lax.axis_index("c"), lax.axis_index("y")
    zl = lax.axis_index("zl")
    z = 2 * lax.axis_index("zh") + zl

    def start(first, second, parity):
        for layer in order:
            for i, offset in enumerate(OFFSETS):
                if layer % 2 == 0:
                    there = lax.rem(y - offset + 2 * RING, RING)
                    pltpu.make_async_copy(
                        half(first, i, layer // 2),
                        w.at[layer, there // 2, lax.rem(there, 2)],
                        sems.at[layer],
                    ).start()
                elif (parity + offset) % 2 == layer // 2:
                    there = lax.rem(z - offset + 2 * RING, RING)
                    for low in range(2):
                        pltpu.make_async_copy(
                            half(second, i, low),
                            w.at[layer, :, low, there // 2],
                            sems.at[layer],
                        ).start()

    for core in range(C):
        for parity in range(ZL):

            @pl.when((c == core) & (zl == parity))
            def _():
                mine, others = pieces[:PIECES], pieces[PIECES:]
                first, second = (mine, others) if core == 0 else (others, mine)
                start(first, second, parity)


def wait_weights(w, sems, layer):
    pltpu.make_async_copy(w.at[layer], w.at[layer], sems.at[layer]).wait()


def head(block, index):
    return block[:, index * HEAD : (index + 1) * HEAD]


def stacked(block, group):
    return jnp.concatenate([head(block, group * GROUPS + a) for a in range(GROUPS)], axis=0)


def unstacked(blocks, length):
    return jnp.concatenate(
        [o[a * length : (a + 1) * length] for o in blocks for a in range(GROUPS)], axis=1
    )


def matmul(a, b, dims):
    return lax.dot_general(a, b, (dims, ((), ())), preferred_element_type=F32)


def forward_kernel(x_ref, gain_ref, mask_ref, *rest):
    w, y_ref, xs_ref, h_ref, kv_ref, p_ref = rest
    length, width = x_ref.shape
    y_ref[...] = x_ref[...]

    @pl.loop(0, LAYERS)
    def _(layer):
        x = y_ref[...]
        xs_ref[layer] = x
        xf = x.astype(F32)
        scale = lax.rsqrt(jnp.mean(xf * xf, axis=-1, keepdims=True) + 1e-05)
        h = (xf * scale * gain_ref[layer]).astype(BF16)
        h_ref[layer] = h
        whole = w[layer].reshape(width, -1)
        kv = matmul(h, whole, ((1,), (0,))).astype(BF16)
        kv_ref[layer] = kv
        groups = range(KV_HEADS)
        s = [matmul(head(kv, g), stacked(h, g), ((1,), (1,))) for g in groups]
        s = jnp.concatenate(s, axis=1)
        s = jnp.where(mask_ref[...] > 0, s * HEAD ** (-0.5), -1e30)
        e = jnp.exp(s - jnp.max(s, axis=0, keepdims=True))
        p = e / jnp.sum(e, axis=0, keepdims=True)
        p_ref[layer] = p
        pb = p.astype(BF16)
        o = [matmul(head(pb, g), head(kv, KV_HEADS + g), ((0,), (0,))) for g in groups]
        y_ref[...] = (xf + unstacked(o, length)).astype(BF16)


def backward_kernel(dy_ref, gain_ref, xs_ref, h_ref, kv_ref, p_ref, *rest):
    w, dx_ref, dkv_ref = rest
    length, width = dy_ref.shape
    dx_ref[...] = dy_ref[...]

    @pl.loop(0, LAYERS)
    def _(turn):
        layer = LAYERS - 1 - turn
        groups = range(KV_HEADS)
        dy, h, kv, p = dx_ref[...], h_ref[layer], kv_ref[layer], p_ref[layer]
        do = [stacked(dy, g) for g in groups]
        pb = p.astype(BF16)
        dv = [matmul(head(pb, g), do[g], ((1,), (0,))) for g in groups]
        dp = [matmul(head(kv, KV_HEADS + g), do[g], ((1,), (1,))) for g in groups]
        dp = jnp.concatenate(dp, axis=1)
        ds = p * (dp - jnp.sum(p * dp, axis=0, keepdims=True)) * HEAD ** (-0.5)
        ds = ds.astype(BF16)
        dk = [matmul(head(ds, g), stacked(h, g), ((1,), (0,))) for g in groups]
        dq = [matmul(head(ds, g), head(kv, g), ((0,), (0,))) for g in groups]
        dkv = jnp.concatenate(dk + dv, axis=1).astype(BF16)
        dkv_ref[layer] = dkv
        whole = w[layer].reshape(width, -1)
        dh = unstacked(dq, length) + matmul(dkv, whole, ((1,), (1,)))
        xf = xs_ref[layer].astype(F32)
        scale = lax.rsqrt(jnp.mean(xf * xf, axis=-1, keepdims=True) + 1e-05)
        gd = dh * gain_ref[layer]
        along = jnp.mean(xf * gd, axis=-1, keepdims=True) * (scale * scale * scale)
        dx_ref[...] = (dy.astype(F32) + (gd * scale - xf * along)).astype(BF16)


VMEM = pl.BlockSpec(memory_space=pltpu.VMEM)
ANY = pl.BlockSpec(memory_space=pl.ANY)
PARAMS = dict(vmem_limit_bytes=16 * 1024 * 1024)


def assemble_kernel(*refs):
    pieces, (w, sems) = refs[: 2 * PIECES], refs[2 * PIECES :]
    fetch_weights(pieces, w, sems, range(LAYERS))
    for layer in range(LAYERS):
        wait_weights(w, sems, layer)


def assembled(pieces):
    rows, columns = pieces[0].shape[1:]
    return pl.pallas_call(
        assemble_kernel,
        out_shape=pltpu.VMEM((LAYERS, Y // 2, 2, ZH, rows, columns), BF16),
        in_specs=[ANY] * (2 * PIECES),
        out_specs=VMEM,
        scratch_shapes=[pltpu.SemaphoreType.DMA((LAYERS,))],
        compiler_params=pltpu.CompilerParams(**PARAMS),
        name="assemble",
    )(*pieces)


def run_forward(x, gains, mask, w):
    length, width = x.shape
    columns = w.shape[-1]
    return pl.pallas_call(
        forward_kernel,
        out_shape=(
            jax.ShapeDtypeStruct((length, width), BF16),
            jax.ShapeDtypeStruct((LAYERS, length, width), BF16),
            jax.ShapeDtypeStruct((LAYERS, length, width), BF16),
            jax.ShapeDtypeStruct((LAYERS, length, columns), BF16),
            jax.ShapeDtypeStruct((LAYERS, length, KV_HEADS * HEAD), F32),
        ),
        in_specs=[VMEM] * 4,
        out_specs=(VMEM,) * 5,
        compiler_params=pltpu.CompilerParams(**PARAMS),
        name="stage_forward",
    )(x, gains, mask, w)


def run_backward(dy, gains, saved, w):
    length, width = dy.shape
    columns = w.shape[-1]
    return pl.pallas_call(
        backward_kernel,
        out_shape=(
            jax.ShapeDtypeStruct((length, width), BF16),
            jax.ShapeDtypeStruct((LAYERS, length, columns), BF16),
        ),
        in_specs=[VMEM] * 7,
        out_specs=(VMEM,) * 2,
        compiler_params=pltpu.CompilerParams(**PARAMS),
        name="stage_backward",
    )(dy, gains, *saved, w)


def exchange(block, axes):
    return lax.all_to_all(block, axes, split_axis=0, concat_axis=0, tiled=True)


def total_of(value):
    for axes, count in ((DP, Y * ZH), (SECTION, X * ZL * C)):
        sent = jnp.broadcast_to(value.reshape(1, 1), (count, 128))
        value = jnp.sum(exchange(sent, axes)[:, 0])
    return value


def body(inputs, upstream, segments, gains, master, moment, second):
    stage = lax.axis_index("x")
    which = lax.axis_index("zl") * C + lax.axis_index("c")
    length, width = inputs.shape[1:]
    rows, columns = master.shape[1:]

    def beside(piece):
        mine, _ = lax.optimization_barrier((gains, piece))
        plane_gains = lax.all_gather(mine, ("zl", "c"), axis=0)
        seg = lax.dynamic_index_in_dim(segments, which, 0, keepdims=False)
        place = jnp.arange(length)
        allowed = (place[None, :] >= place[:, None]) & (seg[None, :] == seg[:, None])
        mask = jnp.tile(allowed.astype(F32), (1, GROUPS * KV_HEADS))
        first = lax.dynamic_index_in_dim(inputs, which, 0, keepdims=False)
        last = lax.dynamic_index_in_dim(upstream, which, 0, keepdims=False)
        is_stage = tuple(stage == i for i in range(X))
        return plane_gains, mask, first, last, is_stage

    pieces, (plane_gains, mask, first, last, is_stage) = gathered_weights(master[0].astype(BF16), beside)
    w = assembled(pieces)

    held = first
    for turn in range(X):
        y, *saved = run_forward(held, plane_gains, mask, w)
        if turn < X - 1:
            arrived = lax.ppermute(y, "x", [(turn, turn + 1)])
            held = jnp.where(is_stage[turn + 1], arrived, held)
        if turn == X - 2:
            h, _ = lax.optimization_barrier((saved[1], arrived))
            early = lax.cond(
                is_stage[X - 1], lambda: jnp.zeros_like(h), lambda: exchange(h, ("zl", "c"))
            )

    held = last
    for turn in range(X):
        here = X - 1 - turn
        dx, dkv = run_backward(held, plane_gains, saved, w)
        if turn < X - 1:
            arrived = lax.ppermute(dx, "x", [(here, here - 1)])
            held = jnp.where(is_stage[here - 1], arrived, held)
        if turn == 0:
            h, _ = lax.optimization_barrier((saved[1], arrived))
            layer_h = lax.cond(
                is_stage[X - 1], lambda: exchange(h, ("zl", "c")), lambda: early
            )
            all_h = lax.all_gather(
                layer_h.reshape(LAYERS * length, width), "y", axis=0, tiled=True
            )

    sent = dkv.reshape(LAYERS, length, Y, columns // Y).transpose(0, 2, 1, 3)
    sent = sent.reshape(LAYERS * Y, length, columns // Y)
    got = exchange(sent, ("zl", "c", "y")).reshape(LAYERS, Y, length, columns // Y)
    tokens = got.transpose(1, 0, 2, 3).reshape(Y * LAYERS * length, columns // Y)
    partial = lax.dot_general(
        all_h, tokens, (((0,), (0,)), ((), ())), preferred_element_type=F32
    ).astype(BF16)
    got = exchange(partial.reshape(Y * ZH, rows, columns // Y), DP)
    grad = jnp.sum(got.reshape(Y, ZH, rows, columns // Y).astype(F32), axis=1)
    grad = grad.transpose(1, 0, 2).reshape(rows, columns)

    total = total_of(jnp.sum(grad * grad))
    entries = X * ZL * C * Y * ZH * grad.size
    factor = jnp.minimum(1.0, 0.01 / jnp.sqrt(total / entries))
    scaled = grad * factor
    new_moment = 0.9 * moment[0] + 0.1 * scaled
    new_second = 0.95 * second[0] + 0.05 * scaled * scaled
    new_master = master[0] - 0.002 * new_moment / (jnp.sqrt(new_second) + 1e-08)
    sections = X * ZL * C
    route = [((i + 1) % sections, i) for i in range(sections)]
    replica = lax.ppermute(new_master.astype(BF16), SECTION, route)
    return (new_master[None], new_moment[None], new_second[None], replica[None])


def solution(mesh):
    fine = Mesh(mesh.devices.reshape(X, ZL, C, Y, ZH), AXES)
    state = P(SECTION, DP, None)
    return jax.shard_map(
        body,
        mesh=fine,
        in_specs=(
            P(None, DP, None),
            P(None, DP, None),
            P(None, DP),
            P(SECTION, None),
            state,
            state,
            state,
        ),
        out_specs=(state,) * 4,
        check_vma=False,
    )
```

```python
import functools

import jax
import jax.numpy as jnp
from jax import lax
from jax.experimental import pallas as pl
from jax.experimental.pallas import tpu as pltpu
from jax.sharding import Mesh
from jax.sharding import PartitionSpec as P

HEAD = 128
X, ZL, C, Y, ZH = 4, 2, 2, 8, 4
AXES = ("x", "zl", "c", "y", "zh")
SECTION = ("x", "zl", "c")
DP = ("y", "zh")
LAYERS = ZL * C
RING = 8
PIECES = RING + 1
HALF = RING // 2
OFFSETS = (0, 1, -1, 2, -2, 3, -3, 4)
KV_HEADS = 4
GROUPS = 4
F32 = jnp.float32
BF16 = jnp.bfloat16


def flat(x, zl, c, y, zh):
    return (((x * ZL + zl) * C + c) * Y + y) * ZH + zh


def everywhere(target):
    pairs = []
    for x in range(X):
        for zl in range(ZL):
            for c in range(C):
                for y in range(Y):
                    for zh in range(ZH):
                        pairs.append((flat(x, zl, c, y, zh), flat(*target(x, zl, c, y, zh))))
    return pairs


def swap_route(bit):
    def target(x, zl, c, y, zh):
        if c == 1:
            return (x, zl, c, y ^ (1 << bit), zh)
        if bit == 0:
            return (x, zl ^ 1, c, y, zh)
        return (x, zl, c, y, zh ^ (1 << (bit - 1)))

    return everywhere(target)


def ring_route(step):
    def target(x, zl, c, y, zh):
        if c == 0:
            return (x, zl, c, (y + step) % Y, zh)
        z = (2 * zh + zl + step) % (ZL * ZH)
        return (x, z % 2, c, y, z // 2)

    return everywhere(target)


def line_groups():
    def place(zl, c, y, zh):
        return flat(0, zl, c, y, zh)

    along_y = [[place(zl, 0, y, zh) for y in range(Y)] for zl in range(ZL) for zh in range(ZH)]
    along_z = [[place(z % 2, 1, y, z // 2) for z in range(RING)] for y in range(Y)]
    return along_y + along_z


def first_gather(master):
    own = master[0].astype(BF16)
    c, y = lax.axis_index("c"), lax.axis_index("y")
    zl, zh = lax.axis_index("zl"), lax.axis_index("zh")
    rows, cols = own.shape
    bits = (
        jnp.where(c == 1, y // 4, zh // 2),
        jnp.where(c == 1, (y // 2) % 2, zh % 2),
        jnp.where(c == 1, y % 2, zl),
    )
    piece = own[None]
    for bit, mine, axis in ((2, bits[0], 0), (1, bits[1], 1), (0, bits[2], 0)):
        other = lax.ppermute(piece, AXES, swap_route(bit))
        low, high = jnp.where(mine == 0, piece, other), jnp.where(mine == 0, other, piece)
        if axis == 0:
            piece = jnp.concatenate([low, high], axis=0)
        else:
            piece = jnp.stack([low, high], axis=1).reshape(-1, rows, cols)
    return piece


def line_gather(piece):
    return lax.all_gather(
        piece[:HALF], "r", axis=0, tiled=True, axis_index_groups=line_groups()
    )


def other_core(block):
    return lax.ppermute(block, "c", [(0, 1), (1, 0)])


def ring_gather(piece, lower, beside):
    pieces, others = [piece[HALF:]], []
    arrived = [pieces[0]] * 2
    for step in range(1, 4):
        up = lax.ppermute(arrived[0], AXES, ring_route(1))
        down = lax.ppermute(arrived[1], AXES, ring_route(-1))
        news = [other_core(p) for p in pieces[len(others) :]]
        if step == 1:
            up, down, news, ready = lax.optimization_barrier((up, down, news, beside(piece)))
        else:
            up, down, news = lax.optimization_barrier((up, down, news))
        others += news
        arrived = [up, down]
        pieces += arrived
    last = lax.ppermute(up, AXES, ring_route(1))
    lower, _ = lax.optimization_barrier((lower, down))
    news = [other_core(p) for p in pieces[len(others) :]]
    lower_other = other_core(lower)
    last, news, lower_other = lax.optimization_barrier((last, news, lower_other))
    others += [*news, other_core(last)]
    pieces.append(last)
    return [lower, *pieces], [lower_other, *others], ready


def assemble_kernel(*refs):
    pieces, (w, sem) = refs[: 2 * PIECES], refs[2 * PIECES :]
    y = lax.axis_index("y")
    z = 2 * lax.axis_index("zh") + lax.axis_index("zl")

    def start(first, second):
        pltpu.make_async_copy(first[0], w.at[0], sem).start()
        for high in range(ZH):
            for low in range(ZL):
                source = second[0].at[high, low]
                pltpu.make_async_copy(source, w.at[2 * low + 1, :, 0, high], sem).start()
        for i, offset in enumerate(OFFSETS):
            there = lax.rem(y - offset + 2 * RING, RING)
            target = w.at[2, there // 2, lax.rem(there, 2)]
            pltpu.make_async_copy(first[1 + i], target, sem).start()
            there = lax.rem(z - offset + 2 * RING, RING)
            target = w.at[2 * lax.rem(there, 2) + 1, :, 1, there // 2]
            pltpu.make_async_copy(second[1 + i], target, sem).start()

    mine, others = pieces[:PIECES], pieces[PIECES:]
    c = lax.axis_index("c")
    pl.when(c == 0)(functools.partial(start, mine, others))
    pl.when(c == 1)(functools.partial(start, others, mine))
    pltpu.make_async_copy(w, w, sem).wait()


def head(block, index):
    return block[:, index * HEAD : (index + 1) * HEAD]


def stacked(block, group):
    return jnp.concatenate([head(block, group * GROUPS + a) for a in range(GROUPS)], axis=0)


def unstacked(blocks, length):
    return jnp.concatenate(
        [o[a * length : (a + 1) * length] for o in blocks for a in range(GROUPS)], axis=1
    )


def matmul(a, b, dims):
    return lax.dot_general(a, b, (dims, ((), ())), preferred_element_type=F32)


def forward_kernel(x_ref, gain_ref, mask_ref, *rest):
    w, y_ref, xs_ref, h_ref, kv_ref, p_ref = rest
    length, width = x_ref.shape
    y_ref[...] = x_ref[...]

    @pl.loop(0, LAYERS)
    def _(layer):
        x = y_ref[...]
        xs_ref[layer] = x
        xf = x.astype(F32)
        scale = lax.rsqrt(jnp.mean(xf * xf, axis=-1, keepdims=True) + 1e-05)
        h = (xf * scale * gain_ref[layer]).astype(BF16)
        h_ref[layer] = h
        whole = w[layer].reshape(width, -1)
        kv = matmul(h, whole, ((1,), (0,))).astype(BF16)
        kv_ref[layer] = kv
        groups = range(KV_HEADS)
        s = [matmul(head(kv, g), stacked(h, g), ((1,), (1,))) for g in groups]
        s = jnp.concatenate(s, axis=1)
        s = jnp.where(mask_ref[...] > 0, s * HEAD ** (-0.5), -1e30)
        e = jnp.exp(s - jnp.max(s, axis=0, keepdims=True))
        p = e / jnp.sum(e, axis=0, keepdims=True)
        p_ref[layer] = p
        pb = p.astype(BF16)
        o = [matmul(head(pb, g), head(kv, KV_HEADS + g), ((0,), (0,))) for g in groups]
        y_ref[...] = (xf + unstacked(o, length)).astype(BF16)


def backward_kernel(dy_ref, gain_ref, xs_ref, h_ref, kv_ref, p_ref, *rest):
    w, dx_ref, dkv_ref = rest
    length, width = dy_ref.shape
    dx_ref[...] = dy_ref[...]

    @pl.loop(0, LAYERS)
    def _(turn):
        layer = LAYERS - 1 - turn
        groups = range(KV_HEADS)
        dy, h, kv, p = dx_ref[...], h_ref[layer], kv_ref[layer], p_ref[layer]
        do = [stacked(dy, g) for g in groups]
        pb = p.astype(BF16)
        dv = [matmul(head(pb, g), do[g], ((1,), (0,))) for g in groups]
        dp = [matmul(head(kv, KV_HEADS + g), do[g], ((1,), (1,))) for g in groups]
        dp = jnp.concatenate(dp, axis=1)
        ds = p * (dp - jnp.sum(p * dp, axis=0, keepdims=True)) * HEAD ** (-0.5)
        ds = ds.astype(BF16)
        dk = [matmul(head(ds, g), stacked(h, g), ((1,), (0,))) for g in groups]
        dq = [matmul(head(ds, g), head(kv, g), ((0,), (0,))) for g in groups]
        dkv = jnp.concatenate(dk + dv, axis=1).astype(BF16)
        dkv_ref[layer] = dkv
        whole = w[layer].reshape(width, -1)
        dh = unstacked(dq, length) + matmul(dkv, whole, ((1,), (1,)))
        xf = xs_ref[layer].astype(F32)
        scale = lax.rsqrt(jnp.mean(xf * xf, axis=-1, keepdims=True) + 1e-05)
        gd = dh * gain_ref[layer]
        along = jnp.mean(xf * gd, axis=-1, keepdims=True) * (scale * scale * scale)
        dx_ref[...] = (dy.astype(F32) + (gd * scale - xf * along)).astype(BF16)


VMEM = pl.BlockSpec(memory_space=pltpu.VMEM)
ANY = pl.BlockSpec(memory_space=pl.ANY)
PARAMS = dict(vmem_limit_bytes=8 * 1024 * 1024)


def assembled(pieces):
    rows, columns = pieces[0].shape[-2:]
    return pl.pallas_call(
        assemble_kernel,
        out_shape=pltpu.VMEM((LAYERS, Y // 2, 2, ZH, rows, columns), BF16),
        in_specs=[ANY] * (2 * PIECES),
        out_specs=VMEM,
        scratch_shapes=[pltpu.SemaphoreType.DMA],
        compiler_params=pltpu.CompilerParams(vmem_limit_bytes=2 * 1024 * 1024),
        name="assemble",
    )(*pieces)


def run_forward(x, gains, mask, w):
    length, width = x.shape
    columns = w.shape[-1]
    return pl.pallas_call(
        forward_kernel,
        out_shape=(
            jax.ShapeDtypeStruct((length, width), BF16),
            jax.ShapeDtypeStruct((LAYERS, length, width), BF16),
            jax.ShapeDtypeStruct((LAYERS, length, width), BF16),
            jax.ShapeDtypeStruct((LAYERS, length, columns), BF16),
            jax.ShapeDtypeStruct((LAYERS, length, KV_HEADS * HEAD), F32),
        ),
        in_specs=[VMEM] * 4,
        out_specs=(VMEM,) * 5,
        compiler_params=pltpu.CompilerParams(**PARAMS),
        name="stage_forward",
    )(x, gains, mask, w)


def run_backward(dy, gains, saved, w):
    length, width = dy.shape
    columns = w.shape[-1]
    return pl.pallas_call(
        backward_kernel,
        out_shape=(
            jax.ShapeDtypeStruct((length, width), BF16),
            jax.ShapeDtypeStruct((LAYERS, length, columns), BF16),
        ),
        in_specs=[VMEM] * 7,
        out_specs=(VMEM,) * 2,
        compiler_params=pltpu.CompilerParams(**PARAMS),
        name="stage_backward",
    )(dy, gains, *saved, w)


def exchange(block, axes):
    return lax.all_to_all(block, axes, split_axis=0, concat_axis=0, tiled=True)


def total_of(value):
    for axes, count in ((DP, Y * ZH), (SECTION, X * ZL * C)):
        sent = jnp.broadcast_to(value.reshape(1, 1), (count, 128))
        value = jnp.sum(exchange(sent, axes)[:, 0])
    return value


def body(piece, lower, inputs, upstream, segments, gains, master, moment, second):
    stage = lax.axis_index("x")
    which = lax.axis_index("zl") * C + lax.axis_index("c")
    length, width = inputs.shape[1:]
    rows, columns = master.shape[1:]

    def beside(piece):
        mine, _ = lax.optimization_barrier((gains, piece))
        plane_gains = lax.all_gather(mine, ("zl", "c"), axis=0)
        seg = lax.dynamic_index_in_dim(segments, which, 0, keepdims=False)
        place = jnp.arange(length)
        allowed = (place[None, :] >= place[:, None]) & (seg[None, :] == seg[:, None])
        mask = jnp.tile(allowed.astype(F32), (1, GROUPS * KV_HEADS))
        first = lax.dynamic_index_in_dim(inputs, which, 0, keepdims=False)
        last = lax.dynamic_index_in_dim(upstream, which, 0, keepdims=False)
        is_stage = tuple(stage == i for i in range(X))
        return plane_gains, mask, first, last, is_stage

    lower = lower.reshape(Y // 2, 2, HALF, rows, columns)
    mine, others, ready = ring_gather(piece, lower, beside)
    plane_gains, mask, first, last, is_stage = ready
    w = assembled([*mine, *others])

    held = first
    for turn in range(X):
        y, *saved = run_forward(held, plane_gains, mask, w)
        if turn < X - 1:
            arrived = lax.ppermute(y, "x", [(turn, turn + 1)])
            held = jnp.where(is_stage[turn + 1], arrived, held)
        if turn == X - 2:
            h, _ = lax.optimization_barrier((saved[1], arrived))
            early = lax.cond(
                is_stage[X - 1], lambda: jnp.zeros_like(h), lambda: exchange(h, ("zl", "c"))
            )

    held = last
    for turn in range(X):
        here = X - 1 - turn
        dx, dkv = run_backward(held, plane_gains, saved, w)
        if turn < X - 1:
            arrived = lax.ppermute(dx, "x", [(here, here - 1)])
            held = jnp.where(is_stage[here - 1], arrived, held)
        if turn == 0:
            h, _ = lax.optimization_barrier((saved[1], arrived))
            layer_h = lax.cond(
                is_stage[X - 1], lambda: exchange(h, ("zl", "c")), lambda: early
            )
            all_h = lax.all_gather(
                layer_h.reshape(LAYERS * length, width), "y", axis=0, tiled=True
            )

    sent = dkv.reshape(LAYERS, length, Y, columns // Y).transpose(0, 2, 1, 3)
    sent = sent.reshape(LAYERS * Y, length, columns // Y)
    got = exchange(sent, ("zl", "c", "y")).reshape(LAYERS, Y, length, columns // Y)
    tokens = got.transpose(1, 0, 2, 3).reshape(Y * LAYERS * length, columns // Y)
    partial = lax.dot_general(
        all_h, tokens, (((0,), (0,)), ((), ())), preferred_element_type=F32
    ).astype(BF16)
    got = exchange(partial.reshape(Y * ZH, rows, columns // Y), DP)
    grad = jnp.sum(got.reshape(Y, ZH, rows, columns // Y).astype(F32), axis=1)
    grad = grad.transpose(1, 0, 2).reshape(rows, columns)

    total = total_of(jnp.sum(grad * grad))
    entries = X * ZL * C * Y * ZH * grad.size
    factor = jnp.minimum(1.0, 0.01 / jnp.sqrt(total / entries))
    scaled = grad * factor
    new_moment = 0.9 * moment[0] + 0.1 * scaled
    new_second = 0.95 * second[0] + 0.05 * scaled * scaled
    new_master = master[0] - 0.002 * new_moment / (jnp.sqrt(new_second) + 1e-08)
    sections = X * ZL * C
    route = [((i + 1) % sections, i) for i in range(sections)]
    replica = lax.ppermute(new_master.astype(BF16), SECTION, route)
    return (new_master[None], new_moment[None], new_second[None], replica[None])


def solution(mesh):
    fine = Mesh(mesh.devices.reshape(X, ZL, C, Y, ZH), AXES)
    lines = Mesh(mesh.devices.reshape(X, ZL * C * Y * ZH), ("x", "r"))
    state = P(SECTION, DP, None)
    each, each_line = P(AXES), P(("x", "r"))
    first = jax.shard_map(
        first_gather, mesh=fine, in_specs=(state,), out_specs=each, check_vma=False
    )
    second = jax.shard_map(
        line_gather, mesh=lines, in_specs=(each_line,), out_specs=each_line, check_vma=False
    )
    rest = jax.shard_map(
        body,
        mesh=fine,
        in_specs=(
            each,
            each,
            P(None, DP, None),
            P(None, DP, None),
            P(None, DP),
            P(SECTION, None),
            state,
            state,
            state,
        ),
        out_specs=(state,) * 4,
        check_vma=False,
    )

    def program(inputs, upstream, segments, gains, master, moment, second_moment):
        piece = first(master)
        return rest(
            piece,
            second(piece),
            inputs,
            upstream,
            segments,
            gains,
            master,
            moment,
            second_moment,
        )

    return program
```
